512 devices in a mesh: head: 2 (over y_hi), inner: 16 (over x, y_lo, core), outer: 16 (over z).
Axes of the slice: x: 4, y: 4 (y_hi: 2, y_lo: 2; y = y_hi * 2 + y_lo), z: 16, core: 2. Of those that a mesh axis runs over, the one named last changes fastest.
Arguments:
- query: bfloat16 [16, 16, 256, 4096], P('outer', 'inner', 'head'), may hold values from -300 to 300
- dout: bfloat16 [16, 16, 256, 4096], P('outer', 'inner', 'head'), may hold values from -6 to 6
- key_mant: bfloat16 [16, 16, 256, 512], P('outer', 'inner', None, 'head'), may hold values from -6 to 6
- value_mantissas: bfloat16 [16, 16, 256, 512], P('outer', 'inner', None, 'head'), may hold values from -6 to 6
- key_exps: int32 [16, 16, 2, 4], P('outer', 'inner', None, 'head'), may hold values from -1 to 1
- value_exponents: int32 [16, 16, 2, 4], P('outer', 'inner', None, 'head'), may hold values from -1 to 1
- reach: int32 [16, 16], P('outer', 'inner'), may hold values from 64 to 256
Outputs:
- query_grad: bfloat16 [16, 16, 256, 4096], P('outer', 'inner', 'head')
- key_grad: bfloat16 [16, 16, 256, 512], P('outer', 'inner', None, 'head')
- value_grad: bfloat16 [16, 16, 256, 512], P('outer', 'inner', None, 'head')
The draws below stay inside these ranges and needn't reach their ends.
All inputs are finite; a program needn't handle non-finite values.
Results may differ from the reference program's by a relative error of at most 0.013.
Values may be sent and summed in bfloat16 or wider, within the bound.
No kernel may reach another device: no remote copies, remote signals or barrier semaphores. Data moves between devices by JAX's collectives and lax.ppermute only.
A program may use at most 64 MiB of HBM per device.

```python
import jax
import jax.numpy as jnp
from jax import lax

QUERY_HEADS = 32
KEY_VALUE_HEADS = 4
HEAD_SIZE = 128
ROWS_PER_SCALE = 128
BLOCK_TOKENS = 256
BLOCKS_PER_GROUP = 16
BLOCK_GROUPS = 16


def shared_keys(key):
    mantissa_values = jax.random.truncated_normal(jax.random.fold_in(key, 101), -6.0, 6.0, (BLOCK_GROUPS, BLOCKS_PER_GROUP, BLOCK_TOKENS, KEY_VALUE_HEADS * HEAD_SIZE), jnp.float32)
    scale_exponents = jax.random.randint(jax.random.fold_in(key, 102), (BLOCK_GROUPS, BLOCKS_PER_GROUP, BLOCK_TOKENS // ROWS_PER_SCALE, KEY_VALUE_HEADS), -1, 2)
    return (mantissa_values, scale_exponents)


def draw_key_exps(key, part):
    mantissa_values, scale_exponents = shared_keys(key)
    return scale_exponents.astype(jnp.int32)


def draw_key_mant(key, part):
    mantissa_values, scale_exponents = shared_keys(key)
    return mantissa_values.astype(jnp.bfloat16)


def draw_query(key, part):
    key = jax.random.fold_in(key, 7)
    block_values = jax.random.truncated_normal(jax.random.fold_in(key, 1), -6.0, 6.0, (BLOCK_GROUPS, BLOCKS_PER_GROUP, BLOCK_TOKENS, QUERY_HEADS * HEAD_SIZE), jnp.float32)
    return block_values.astype(jnp.bfloat16)


def place_ends(drawn, key, least, largest):
    dims = drawn.shape
    spot = [jax.random.randint(jax.random.fold_in(key, axis), (), 0, dims[axis]) for axis in range(len(dims))]
    drawn = drawn.at[tuple(spot)].set(least)
    longest = dims.index(max(dims))
    spot[longest] = (spot[longest] + 1) % dims[longest]
    return drawn.at[tuple(spot)].set(largest)


def steps_of(rng, shape, shards, low, top_value):
    gain, own = 1.0, jax.random.fold_in(rng, 6)
    for axis_at, blocks in shards:
        heights = jnp.exp(jax.random.uniform(jax.random.fold_in(own, axis_at), (blocks,), jnp.float32, low / len(shards), top_value / len(shards)))
        gain = gain * jnp.repeat(heights, shape[axis_at] // blocks).reshape([-1 if axis == axis_at else 1 for axis in range(len(shape))])
    return gain


def centred(stream_key, shape, spread, most, cuts=(), dtype=jnp.bfloat16):
    level = steps_of(stream_key, shape, cuts, -0.22, 0.18) if cuts else 1.0
    result = jax.random.normal(stream_key, shape, jnp.float32) * spread * level
    return jnp.minimum(jnp.maximum(result, -most), most).astype(dtype)


def setup_inputs(seed: int = 0) -> dict:
    key_list = jax.random.split(jax.random.key(seed), 8)
    return {
        "query": draw_query(jax.random.fold_in(key_list[7], 71), 0),
        "dout": centred(key_list[1], (BLOCK_GROUPS, BLOCKS_PER_GROUP, BLOCK_TOKENS, QUERY_HEADS * HEAD_SIZE), 1.0, 6.0, ((0, 16), (1, 16), (2, 2))),
        "key_mant": draw_key_mant(jax.random.fold_in(key_list[7], 71), 0),
        "value_mantissas": centred(key_list[3], (BLOCK_GROUPS, BLOCKS_PER_GROUP, BLOCK_TOKENS, KEY_VALUE_HEADS * HEAD_SIZE), 1.0, 6.0, ((0, 16), (1, 16), (3, 2))),
        "key_exps": draw_key_exps(jax.random.fold_in(key_list[7], 71), 0),
        "value_exponents": place_ends(jax.random.randint(key_list[5], (BLOCK_GROUPS, BLOCKS_PER_GROUP, BLOCK_TOKENS // ROWS_PER_SCALE, KEY_VALUE_HEADS), -1, 2), jax.random.fold_in(key_list[5], 1), -1, 1).astype(jnp.int32),
        "reach": place_ends(jax.random.randint(key_list[6], (BLOCK_GROUPS, BLOCKS_PER_GROUP), BLOCK_TOKENS // 4, BLOCK_TOKENS + 1), jax.random.fold_in(key_list[6], 1), BLOCK_TOKENS // 4, BLOCK_TOKENS).astype(jnp.int32),
    }


NEG_FILL = -1e30


def dequant(mantissa_values, scale_exponents):
    reshaped_array = mantissa_values.astype(jnp.float32).reshape(BLOCK_GROUPS, BLOCKS_PER_GROUP, BLOCK_TOKENS // ROWS_PER_SCALE, ROWS_PER_SCALE, KEY_VALUE_HEADS, HEAD_SIZE)
    scale_factors = jnp.exp2(scale_exponents.astype(jnp.float32))[:, :, :, None, :, None]
    return (reshaped_array * scale_factors).astype(jnp.bfloat16).reshape(BLOCK_GROUPS, BLOCKS_PER_GROUP, BLOCK_TOKENS, KEY_VALUE_HEADS, HEAD_SIZE)


def one_block(members):
    query_matrix, gradient_rows, key_own, value_own, key_prev, value_prev, reach_rows, first_cycle = members
    heads_per_group = QUERY_HEADS // KEY_VALUE_HEADS
    factor = HEAD_SIZE ** -0.5
    query_complete = query_matrix.reshape(BLOCK_TOKENS, KEY_VALUE_HEADS, heads_per_group, HEAD_SIZE).astype(jnp.float32)
    gradient_complete = gradient_rows.reshape(BLOCK_TOKENS, KEY_VALUE_HEADS, heads_per_group, HEAD_SIZE).astype(jnp.float32)
    key_all = jnp.concatenate([key_prev, key_own], axis=0).astype(jnp.float32)
    value_all = jnp.concatenate([value_prev, value_own], axis=0).astype(jnp.float32)
    scores = jnp.einsum("tkgd,skd->kgts", query_complete, key_all) * factor
    columns = jnp.arange(2 * BLOCK_TOKENS)
    positions = jnp.arange(BLOCK_TOKENS)
    prev_mask = (columns < BLOCK_TOKENS) & (columns >= BLOCK_TOKENS - reach_rows) & jnp.logical_not(first_cycle)
    own_mask = (columns[None, :] >= BLOCK_TOKENS) & (columns[None, :] - BLOCK_TOKENS <= positions[:, None])
    visible = own_mask | prev_mask[None, :]
    scores = jnp.where(visible[None, None], scores, NEG_FILL)
    row_peak = jnp.max(scores, axis=3, keepdims=True)
    weights = jnp.exp(scores - row_peak)
    probs = weights / jnp.sum(weights, axis=3, keepdims=True)
    rounded = lax.optimization_barrier(probs.astype(jnp.bfloat16)).astype(jnp.float32)
    output = jnp.einsum("kgts,skd->kgtd", rounded, value_all)
    row_dot = jnp.einsum("tkgd,kgtd->kgt", gradient_complete, output)
    dprob = jnp.einsum("tkgd,skd->kgts", gradient_complete, value_all)
    dscore = lax.optimization_barrier((probs * (dprob - row_dot[..., None])).astype(jnp.bfloat16)).astype(jnp.float32)
    query_grad = (jnp.einsum("kgts,skd->tkgd", dscore, key_all) * factor).astype(jnp.bfloat16)
    key_terms = jnp.einsum("kgts,tkgd->skd", dscore, query_complete) * factor
    value_terms = jnp.einsum("kgts,tkgd->skd", rounded, gradient_complete)
    return (query_grad.reshape(BLOCK_TOKENS, QUERY_HEADS * HEAD_SIZE), key_terms[BLOCK_TOKENS:], value_terms[BLOCK_TOKENS:],
            key_terms[:BLOCK_TOKENS], value_terms[:BLOCK_TOKENS])


def reference(query, dout, key_mant, value_mantissas, key_exps, value_exponents, reach):
    block_keys = dequant(key_mant, key_exps)
    block_values = dequant(value_mantissas, value_exponents)
    predecessor_keys = jnp.concatenate([jnp.zeros_like(block_keys[:, :1]), block_keys[:, :-1]], axis=1)
    predecessor_values = jnp.concatenate([jnp.zeros_like(block_values[:, :1]), block_values[:, :-1]], axis=1)
    first_flags = jnp.broadcast_to(jnp.arange(BLOCKS_PER_GROUP)[None, :] == 0, (BLOCK_GROUPS, BLOCKS_PER_GROUP))
    item_count = BLOCK_GROUPS * BLOCKS_PER_GROUP
    members = (query.reshape(item_count, BLOCK_TOKENS, QUERY_HEADS * HEAD_SIZE), dout.reshape(item_count, BLOCK_TOKENS, QUERY_HEADS * HEAD_SIZE),
               block_keys.reshape(item_count, BLOCK_TOKENS, KEY_VALUE_HEADS, HEAD_SIZE), block_values.reshape(item_count, BLOCK_TOKENS, KEY_VALUE_HEADS, HEAD_SIZE),
               predecessor_keys.reshape(item_count, BLOCK_TOKENS, KEY_VALUE_HEADS, HEAD_SIZE), predecessor_values.reshape(item_count, BLOCK_TOKENS, KEY_VALUE_HEADS, HEAD_SIZE),
               reach.reshape(item_count), first_flags.reshape(item_count))
    query_grad, key_own, value_own, key_next, value_next = lax.map(one_block, members)
    key_value_shape = (BLOCK_GROUPS, BLOCKS_PER_GROUP, BLOCK_TOKENS, KEY_VALUE_HEADS, HEAD_SIZE)
    key_next = lax.optimization_barrier(key_next.reshape(key_value_shape).astype(jnp.bfloat16)).astype(jnp.float32)
    value_next = lax.optimization_barrier(value_next.reshape(key_value_shape).astype(jnp.bfloat16)).astype(jnp.float32)
    key_next = jnp.concatenate([key_next[:, 1:], jnp.zeros_like(key_next[:, :1])], axis=1)
    value_next = jnp.concatenate([value_next[:, 1:], jnp.zeros_like(value_next[:, :1])], axis=1)
    key_grad = (key_own.reshape(key_value_shape) + key_next).astype(jnp.bfloat16)
    value_grad = (value_own.reshape(key_value_shape) + value_next).astype(jnp.bfloat16)
    output_shape = (BLOCK_GROUPS, BLOCKS_PER_GROUP, BLOCK_TOKENS, KEY_VALUE_HEADS * HEAD_SIZE)
    return (query_grad.reshape(BLOCK_GROUPS, BLOCKS_PER_GROUP, BLOCK_TOKENS, QUERY_HEADS * HEAD_SIZE), key_grad.reshape(output_shape),
            value_grad.reshape(output_shape))
```

```python
import functools

import jax
import jax.numpy as jnp
from jax import lax
from jax.experimental import pallas as pl
from jax.experimental.pallas import tpu as pltpu
from jax.sharding import PartitionSpec as P

QUERY_HEADS = 32
KEY_VALUE_HEADS = 4
HEAD_SIZE = 128
ROWS_PER_SCALE = 128
GROUP = QUERY_HEADS // KEY_VALUE_HEADS
FACTOR = HEAD_SIZE**-0.5
LOG2_E = 1.4426950408889634
NEG_FILL = -1e30
PAIR = 2


def nt(a, b):
    return lax.dot_general(a, b, (((1,), (1,)), ((), ())), preferred_element_type=jnp.float32)


def nn(a, b):
    return lax.dot_general(a, b, (((1,), (0,)), ((), ())), preferred_element_type=jnp.float32)


def pack_kernel(key_exps, value_exps, key_ref, value_ref, out_ref):
    length = key_ref.shape[0]
    for source, exps, base in ((key_ref, key_exps, 0), (value_ref, value_exps, length)):
        for run in range(length // ROWS_PER_SCALE):
            rows = slice(run * ROWS_PER_SCALE, (run + 1) * ROWS_PER_SCALE)
            for head in range(source.shape[1] // HEAD_SIZE):
                cols = slice(head * HEAD_SIZE, (head + 1) * HEAD_SIZE)
                exponent = jnp.full((8, HEAD_SIZE), exps[run, head], jnp.int32).astype(jnp.float32)
                scale = jnp.exp2(exponent)[:1]
                out_ref[base + run * ROWS_PER_SCALE : base + (run + 1) * ROWS_PER_SCALE, cols] = (
                    source[rows, cols].astype(jnp.float32) * scale
                ).astype(jnp.bfloat16)


def pack(key_mant, value_mant, key_exps, value_exps):
    length, width = key_mant.shape
    smem = pl.BlockSpec(memory_space=pltpu.SMEM)
    vmem = pl.BlockSpec(memory_space=pltpu.VMEM)
    return pl.pallas_call(
        pack_kernel,
        out_shape=jax.ShapeDtypeStruct((2 * length, width), jnp.bfloat16),
        in_specs=[smem, smem, vmem, vmem],
        out_specs=vmem,
        name="pack",
    )(key_exps, value_exps, key_mant, value_mant)


def attend_kernel(place, q_ref, g_ref, own_ref, prev_ref, *refs):
    dq_ref, next_ref, term_ref = refs[-3:]
    tokens = q_ref.shape[0]
    length = own_ref.shape[0] // 2
    rows = lax.broadcasted_iota(jnp.int32, (2 * length, tokens), 0)
    cols = lax.broadcasted_iota(jnp.int32, (2 * length, tokens), 1)
    last = jnp.where(rows < length, 2 * length, cols + (length + place[1] * tokens))
    visible = jnp.logical_and(rows >= place[2], rows <= last)
    bias = jnp.where(visible, 0.0, NEG_FILL)
    bias = jnp.concatenate([bias] * PAIR, axis=1)
    keys = jnp.concatenate([prev_ref[:length], own_ref[:length]], axis=0)
    values = jnp.concatenate([prev_ref[length:], own_ref[length:]], axis=0)
    keys_t = keys.T
    dk = dv = None
    for start in range(0, GROUP, PAIR):
        spans = [slice(h * HEAD_SIZE, (h + 1) * HEAD_SIZE) for h in range(start, start + PAIR)]
        queries = jnp.concatenate([q_ref[:, s] for s in spans], axis=0)
        grads = jnp.concatenate([g_ref[:, s] for s in spans], axis=0)
        scores = nt(keys, queries) + bias
        dprob = nt(values, grads)
        peak = jnp.max(scores, axis=0, keepdims=True)
        weights = jnp.exp2((scores - peak) * (FACTOR * LOG2_E))
        inverse = 1.0 / jnp.sum(weights, axis=0, keepdims=True)
        row_dot = jnp.sum(weights * dprob, axis=0, keepdims=True) * inverse
        probs = weights * inverse
        dscore = (probs * (dprob - row_dot)).astype(jnp.bfloat16)
        probs = probs.astype(jnp.bfloat16)
        dk_part = nn(dscore, queries)
        dv_part = nn(probs, grads)
        dk = dk_part if dk is None else dk + dk_part
        dv = dv_part if dv is None else dv + dv_part
        dq = (nn(keys_t, dscore) * FACTOR).astype(jnp.bfloat16).T
        for at, s in enumerate(spans):
            dq_ref[:, s] = dq[at * tokens : (at + 1) * tokens]
    dk = dk * FACTOR
    next_ref[:length] = dk[:length].astype(next_ref.dtype)
    next_ref[length:] = dv[:length].astype(next_ref.dtype)
    term_ref[:length] = dk[length:].astype(term_ref.dtype)
    term_ref[length:] = dv[length:].astype(term_ref.dtype)


def attend(place, query, dout, own, prev, dq_so_far, term_dtype, name):
    tokens, width = query.shape
    rows, half = own.shape
    heads = half // HEAD_SIZE
    wide = pl.BlockSpec((tokens, GROUP * HEAD_SIZE), lambda j, s: (0, heads * s[0] + j))
    narrow = pl.BlockSpec((rows, HEAD_SIZE), lambda j, s: (0, j))
    operands = [place, query, dout, own, prev]
    in_specs = [wide, wide, narrow, narrow]
    aliases = {}
    if dq_so_far is not None:
        operands.append(dq_so_far)
        in_specs.append(pl.BlockSpec(memory_space=pl.ANY))
        aliases = {5: 0}
    return pl.pallas_call(
        attend_kernel,
        out_shape=(
            jax.ShapeDtypeStruct((tokens, width), jnp.bfloat16),
            jax.ShapeDtypeStruct((rows, half), jnp.bfloat16),
            jax.ShapeDtypeStruct((rows, half), term_dtype),
        ),
        grid_spec=pltpu.PrefetchScalarGridSpec(
            num_scalar_prefetch=1,
            grid=(heads,),
            in_specs=in_specs,
            out_specs=[wide, narrow, narrow],
        ),
        input_output_aliases=aliases,
        cost_estimate=pl.CostEstimate(
            flops=10 * heads * GROUP * tokens * rows * HEAD_SIZE,
            bytes_accessed=4 * 1024 * 1024,
            transcendentals=heads * GROUP * tokens * rows,
        ),
        compiler_params=pltpu.CompilerParams(vmem_limit_bytes=32 * 1024 * 1024),
        name=name,
    )(*operands)


def on_device(query, dout, key_mant, value_mantissas, key_exps, value_exponents, reach):
    inner = lax.axis_size("inner")
    mine = lax.axis_index("head")
    first = lax.axis_index("inner") == 0
    length = key_mant.shape[2]
    query_rows, dout_rows = query[0, 0], dout[0, 0]
    own = pack(key_mant[0, 0], value_mantissas[0, 0], key_exps[0, 0], value_exponents[0, 0])

    def forward(value):
        return lax.ppermute(value, "inner", [(i, i + 1) for i in range(inner - 1)])

    def backward(value):
        return lax.ppermute(value, "inner", [(i + 1, i) for i in range(inner - 1)])

    def swap(value):
        return lax.ppermute(value, "head", [(0, 1), (1, 0)])

    def across(value, step):
        pairs = [
            (head * inner + at, (1 - head) * inner + at + step)
            for head in range(2)
            for at in range(max(0, -step), min(inner, inner - step))
        ]
        return lax.ppermute(value, ("head", "inner"), pairs)

    prev = forward(own)
    other_own = swap(own)
    other_prev = across(own, 1)
    lowest = jnp.where(first, length, length - reach[0, 0])
    local = jnp.stack([mine, mine, lowest]).astype(jnp.int32)
    remote = jnp.stack([1 - mine, mine, lowest]).astype(jnp.int32)
    dq, next_here, term_here = attend(
        local, query_rows, dout_rows, own, prev, None, jnp.float32, "attend_local"
    )
    returned = backward(next_here)
    dq, next_there, term_there = attend(
        remote, query_rows, dout_rows, other_own, other_prev, dq, jnp.bfloat16, "attend_remote"
    )
    swapped = swap(term_there)
    crossed = across(next_there, -1)
    total = term_here
    for part in (returned, swapped, crossed):
        total = total + part.astype(jnp.float32)
    total = total.astype(jnp.bfloat16)
    return dq[None, None], total[None, None, :length], total[None, None, length:]


def solution(mesh):
    placed = (
        P("outer", "inner", "head", None),
        P("outer", "inner", "head", None),
        P("outer", "inner", None, "head"),
        P("outer", "inner", None, "head"),
        P("outer", "inner", None, "head"),
        P("outer", "inner", None, "head"),
        P("outer", "inner"),
    )
    return jax.shard_map(
        on_device,
        mesh=mesh,
        in_specs=placed,
        out_specs=(
            P("outer", "inner", "head", None),
            P("outer", "inner", None, "head"),
            P("outer", "inner", None, "head"),
        ),
        check_vma=False,
    )
```

```python
import functools

import jax
import jax.numpy as jnp
from jax import lax
from jax.experimental import pallas as pl
from jax.experimental.pallas import tpu as pltpu
from jax.sharding import PartitionSpec as P

QUERY_HEADS = 32
KEY_VALUE_HEADS = 4
HEAD_SIZE = 128
ROWS_PER_SCALE = 128
GROUP = QUERY_HEADS // KEY_VALUE_HEADS
FACTOR = HEAD_SIZE**-0.5
LOG2_E = 1.4426950408889634
NEG_FILL = -1e30
PAIR = 8


def nt(a, b):
    return lax.dot_general(a, b, (((1,), (1,)), ((), ())), preferred_element_type=jnp.float32)


def nn(a, b):
    return lax.dot_general(a, b, (((1,), (0,)), ((), ())), preferred_element_type=jnp.float32)


def in_vmem(shape, dtype):
    return pltpu.VMEM(shape, dtype)


def pinned(value, space):
    return pltpu.with_memory_space_constraint(value, space)


def pack_kernel(
    key_exps, value_exps, reach, key_hbm, value_hbm, q_hbm, g_hbm,
    out_ref, bias_ref, q_ref, g_ref, key_ref, value_ref, sem,
):
    pairs = ((key_hbm, key_ref), (value_hbm, value_ref), (q_hbm, q_ref), (g_hbm, g_ref))
    loads = [pltpu.make_async_copy(*pair, sem.at[at]) for at, pair in enumerate(pairs)]
    for load in loads:
        load.start()
    length = key_ref.shape[0]
    tokens = q_ref.shape[0]
    rows = lax.broadcasted_iota(jnp.int32, (2 * length, tokens), 0)
    cols = lax.broadcasted_iota(jnp.int32, (2 * length, tokens), 1)
    last = jnp.where(rows < length, length, cols + (length + lax.axis_index("head") * tokens))
    lowest = jnp.where(lax.axis_index("inner") == 0, length, length - reach[0, 0])
    visible = jnp.logical_and(rows >= lowest, rows <= last)
    bias_ref[...] = jnp.where(visible, 0.0, NEG_FILL).astype(jnp.bfloat16)
    for load, source, exps, base in (
        (loads[0], key_ref, key_exps, 0),
        (loads[1], value_ref, value_exps, length),
    ):
        load.wait()
        for run in range(length // ROWS_PER_SCALE):
            part = slice(run * ROWS_PER_SCALE, (run + 1) * ROWS_PER_SCALE)
            to = slice(base + part.start, base + part.stop)
            for head in range(source.shape[1] // HEAD_SIZE):
                at = slice(head * HEAD_SIZE, (head + 1) * HEAD_SIZE)
                exponent = jnp.full((8, HEAD_SIZE), exps[run, head], jnp.int32).astype(jnp.float32)
                scale = jnp.exp2(exponent)[:1].astype(jnp.bfloat16)
                out_ref[to, at] = source[part, at] * scale
    for load in loads[2:]:
        load.wait()


def pack(key_mant, value_mant, key_exps, value_exps, reach, query, dout):
    length, width = key_mant.shape
    tokens = query.shape[0]
    smem = pl.BlockSpec(memory_space=pltpu.SMEM)
    vmem = pl.BlockSpec(memory_space=pltpu.VMEM)
    hbm = pl.BlockSpec(memory_space=pltpu.HBM)
    return pl.pallas_call(
        pack_kernel,
        out_shape=(
            in_vmem((2 * length, width), jnp.bfloat16),
            in_vmem((2 * length, tokens), jnp.bfloat16),
            in_vmem(query.shape, jnp.bfloat16),
            in_vmem(dout.shape, jnp.bfloat16),
        ),
        in_specs=[smem] * 3 + [hbm] * 4,
        out_specs=[vmem] * 4,
        scratch_shapes=[
            pltpu.VMEM((length, width), jnp.bfloat16),
            pltpu.VMEM((length, width), jnp.bfloat16),
            pltpu.SemaphoreType.DMA((4,)),
        ],
        compiler_params=pltpu.CompilerParams(vmem_limit_bytes=16 * 1024 * 1024),
        name="pack",
    )(key_exps, value_exps, reach, *(pinned(x, pltpu.HBM) for x in (key_mant, value_mant, query, dout)))


def attend_kernel(remote, bias_ref, q_ref, g_ref, own_ref, prev_ref, *refs):
    dq_hbm, next_ref, term_ref, dq_ref, sem = refs[-5:]
    tokens = q_ref.shape[0]
    length = own_ref.shape[0] // 2
    heads = own_ref.shape[1] // HEAD_SIZE
    wide = GROUP * HEAD_SIZE
    span = PAIR * HEAD_SIZE
    group = lax.axis_index("head")
    base = (1 - group if remote else group) * (heads * wide)
    bias = bias_ref[...]
    ident = (
        lax.broadcasted_iota(jnp.int32, (tokens, tokens), 0)
        == lax.broadcasted_iota(jnp.int32, (tokens, tokens), 1)
    )
    ident = jnp.where(ident, 1.0, 0.0).astype(jnp.bfloat16)
    ident = jnp.concatenate([ident] * PAIR, axis=0)

    def column(head):
        return pl.ds(pl.multiple_of(base + head * HEAD_SIZE, HEAD_SIZE), HEAD_SIZE)

    def stacked(ref, step):
        return jnp.concatenate(
            [ref[:, column(h)] for h in range(step * PAIR, (step + 1) * PAIR)], axis=0
        )

    def keys_of(kv):
        at = slice(kv * HEAD_SIZE, (kv + 1) * HEAD_SIZE)
        return jnp.concatenate([prev_ref[:length, at], own_ref[:length, at]], axis=0)

    def values_of(kv):
        at = slice(kv * HEAD_SIZE, (kv + 1) * HEAD_SIZE)
        return jnp.concatenate([prev_ref[length:, at], own_ref[length:, at]], axis=0)

    def project(step):
        kv = step * PAIR // GROUP
        masked_keys = jnp.concatenate([keys_of(kv), bias], axis=1)
        scores = nt(masked_keys, jnp.concatenate([stacked(q_ref, step), ident], axis=1))
        return scores, nt(values_of(kv), stacked(g_ref, step))

    def soften(scores, dprob):
        peak = jnp.max(scores, axis=0, keepdims=True)
        weights = jnp.exp2((scores - peak) * (FACTOR * LOG2_E))
        inverse = 1.0 / jnp.sum(weights, axis=0, keepdims=True)
        row_dot = jnp.sum(weights * dprob, axis=0, keepdims=True) * inverse
        probs = weights * inverse
        dscore = (probs * (dprob - row_dot)).astype(jnp.bfloat16)
        return probs.astype(jnp.bfloat16), dscore

    def finish(step, dscore):
        kv = step * PAIR // GROUP
        dq = (nn(keys_of(kv).T, dscore) * FACTOR).astype(jnp.bfloat16).T
        for i in range(PAIR):
            h = step * PAIR + i
            dq_ref[:, h * HEAD_SIZE : (h + 1) * HEAD_SIZE] = dq[i * tokens : (i + 1) * tokens]

    def send(kv):
        at = slice(kv * wide, (kv + 1) * wide)
        to = pl.ds(pl.multiple_of(base + kv * wide, HEAD_SIZE), wide)
        return pltpu.make_async_copy(dq_ref.at[:, at], dq_hbm.at[:, to], sem.at[kv])

    def gather(step, probs, dscore):
        return nn(dscore, stacked(q_ref, step)), nn(probs, stacked(g_ref, step))

    def deliver(kv, dk, dv):
        dk = dk * FACTOR
        at = slice(kv * HEAD_SIZE, (kv + 1) * HEAD_SIZE)
        next_ref[:length, at] = dk[:length].astype(next_ref.dtype)
        next_ref[length:, at] = dv[:length].astype(next_ref.dtype)
        term_ref[:length, at] = dk[length:].astype(term_ref.dtype)
        term_ref[length:, at] = dv[length:].astype(term_ref.dtype)

    steps = heads * GROUP // PAIR
    per = GROUP // PAIR
    raw = project(0)
    sums = [[0.0, 0.0] for _ in range(heads)]
    for step in range(steps):
        ahead = project(step + 1) if step + 1 < steps else None
        probs, dscore = soften(*raw)
        raw = ahead
        finish(step, dscore)
        kv = step // per
        parts = gather(step, probs, dscore)
        sums[kv] = [x + y for x, y in zip(sums[kv], parts)]
        if (step + 1) % per == 0:
            send(kv).start()
            deliver(kv, *sums[kv])
    for kv in range(heads):
        send(kv).wait()


def attend(remote, bias, query, dout, own, prev, dq_so_far, term_dtype, name):
    tokens, width = query.shape
    rows, half = own.shape
    heads = half // HEAD_SIZE
    vmem = pl.BlockSpec(memory_space=pltpu.VMEM)
    operands = [pinned(x, pltpu.VMEM) for x in (bias, query, dout, own, prev)]
    in_specs = [vmem] * 5
    aliases = {}
    if dq_so_far is not None:
        operands.append(dq_so_far)
        in_specs.append(pl.BlockSpec(memory_space=pl.ANY))
        aliases = {5: 0}
    lanes = heads * GROUP * HEAD_SIZE
    return pl.pallas_call(
        functools.partial(attend_kernel, remote),
        out_shape=(
            jax.ShapeDtypeStruct((tokens, width), jnp.bfloat16),
            in_vmem((rows, half), jnp.bfloat16),
            in_vmem((rows, half), term_dtype),
        ),
        in_specs=in_specs,
        out_specs=[pl.BlockSpec(memory_space=pl.ANY), vmem, vmem],
        scratch_shapes=[pltpu.VMEM((tokens, lanes), jnp.bfloat16), pltpu.SemaphoreType.DMA((heads,))],
        input_output_aliases=aliases,
        cost_estimate=pl.CostEstimate(
            flops=10 * heads * GROUP * tokens * rows * HEAD_SIZE,
            bytes_accessed=4 * 1024 * 1024,
            transcendentals=heads * GROUP * tokens * rows,
        ),
        compiler_params=pltpu.CompilerParams(vmem_limit_bytes=32 * 1024 * 1024),
        name=name,
    )(*operands)


def on_device(query, dout, key_mant, value_mantissas, key_exps, value_exponents, reach):
    inner = lax.axis_size("inner")
    length = key_mant.shape[2]
    query_rows, dout_rows = query[0, 0], dout[0, 0]
    own, bias, query_rows, dout_rows = pack(
        key_mant[0, 0],
        value_mantissas[0, 0],
        key_exps[0, 0],
        value_exponents[0, 0],
        reach,
        query_rows,
        dout_rows,
    )

    def forward(value):
        return lax.ppermute(value, "inner", [(i, i + 1) for i in range(inner - 1)])

    def backward(value):
        return lax.ppermute(value, "inner", [(i + 1, i) for i in range(inner - 1)])

    def swap(value):
        return lax.ppermute(value, "head", [(0, 1), (1, 0)])

    def across(value, step):
        pairs = [
            (head * inner + at, (1 - head) * inner + at + step)
            for head in range(2)
            for at in range(max(0, -step), min(inner, inner - step))
        ]
        return lax.ppermute(value, ("head", "inner"), pairs)

    prev = forward(own)
    other_own = swap(own)
    other_prev = across(own, 1)
    dq, next_here, term_here = attend(
        False, bias, query_rows, dout_rows, own, prev, None, jnp.float32, "attend_local"
    )
    returned = backward(next_here)
    dq, next_there, term_there = attend(
        True, bias, query_rows, dout_rows, other_own, other_prev, dq, jnp.bfloat16, "attend_remote"
    )
    swapped = swap(term_there)
    crossed = across(next_there, -1)
    total = term_here
    for part in (returned, swapped, crossed):
        total = total + part.astype(jnp.float32)
    total = total.astype(jnp.bfloat16)
    return dq[None, None], total[None, None, :length], total[None, None, length:]


def solution(mesh):
    placed = (
        P("outer", "inner", "head", None),
        P("outer", "inner", "head", None),
        P("outer", "inner", None, "head"),
        P("outer", "inner", None, "head"),
        P("outer", "inner", None, "head"),
        P("outer", "inner", None, "head"),
        P("outer", "inner"),
    )
    return jax.shard_map(
        on_device,
        mesh=mesh,
        in_specs=placed,
        out_specs=(
            P("outer", "inner", "head", None),
            P("outer", "inner", None, "head"),
            P("outer", "inner", None, "head"),
        ),
        check_vma=False,
    )
```

```python
import functools

import jax
import jax.numpy as jnp
from jax import lax
from jax.experimental import pallas as pl
from jax.experimental.pallas import tpu as pltpu
from jax.sharding import PartitionSpec as P

QUERY_HEADS = 32
KEY_VALUE_HEADS = 4
HEAD_SIZE = 128
ROWS_PER_SCALE = 128
GROUP = QUERY_HEADS // KEY_VALUE_HEADS
FACTOR = HEAD_SIZE**-0.5
LOG2_E = 1.4426950408889634
NEG_FILL = -1e30
PAIR = 8
PACK_FLOPS = 8 * 10**9
PACK_VMEM = 48


def nt(a, b):
    return lax.dot_general(a, b, (((1,), (1,)), ((), ())), preferred_element_type=jnp.float32)


def nn(a, b):
    return lax.dot_general(a, b, (((1,), (0,)), ((), ())), preferred_element_type=jnp.float32)


def in_vmem(shape, dtype):
    return pltpu.VMEM(shape, dtype)


def pinned(value, space):
    return pltpu.with_memory_space_constraint(value, space)


def pack_kernel(
    key_exps_hbm, value_exps_hbm, key_hbm, value_hbm, out_ref, key_ref, value_ref, key_exps, value_exps, sem
):
    length = key_ref.shape[0]
    loads = [
        pltpu.make_async_copy(key_hbm, key_ref, sem.at[0]),
        pltpu.make_async_copy(value_hbm, value_ref, sem.at[1]),
        pltpu.make_async_copy(key_exps_hbm, key_exps, sem.at[2]),
        pltpu.make_async_copy(value_exps_hbm, value_exps, sem.at[3]),
    ]
    for load in loads:
        load.start()
    for load in loads[2:]:
        load.wait()
    for load, source, exps, base in (
        (loads[0], key_ref, key_exps, 0),
        (loads[1], value_ref, value_exps, length),
    ):
        load.wait()
        for run in range(length // ROWS_PER_SCALE):
            part = slice(run * ROWS_PER_SCALE, (run + 1) * ROWS_PER_SCALE)
            to = slice(base + part.start, base + part.stop)
            for head in range(source.shape[1] // HEAD_SIZE):
                at = slice(head * HEAD_SIZE, (head + 1) * HEAD_SIZE)
                exponent = jnp.full((8, HEAD_SIZE), exps[run, head], jnp.int32).astype(jnp.float32)
                scale = jnp.exp2(exponent)[:1].astype(jnp.bfloat16)
                out_ref[to, at] = source[part, at] * scale


def pack(key_mant, value_mant, key_exps, value_exps):
    length, width = key_mant.shape
    vmem = pl.BlockSpec(memory_space=pltpu.VMEM)
    hbm = pl.BlockSpec(memory_space=pltpu.HBM)
    return pl.pallas_call(
        pack_kernel,
        out_shape=in_vmem((2 * length, width), jnp.bfloat16),
        in_specs=[hbm] * 4,
        out_specs=vmem,
        scratch_shapes=[
            pltpu.VMEM((length, width), jnp.bfloat16),
            pltpu.VMEM((length, width), jnp.bfloat16),
            pltpu.SMEM(key_exps.shape, jnp.int32),
            pltpu.SMEM(value_exps.shape, jnp.int32),
            pltpu.SemaphoreType.DMA((4,)),
        ],
        cost_estimate=pl.CostEstimate(flops=PACK_FLOPS, bytes_accessed=1024 * 1024, transcendentals=0),
        compiler_params=pltpu.CompilerParams(vmem_limit_bytes=PACK_VMEM * 1024 * 1024),
        name="pack",
    )(*(pinned(x, pltpu.HBM) for x in (key_exps, value_exps, key_mant, value_mant)))


def fetch(reach_hbm, reach_ref, bias_ref, q_ref, sem):
    group = lax.axis_index("head")
    bound = pltpu.make_async_copy(reach_hbm, reach_ref, sem.at[0])
    bound.start()
    tokens = q_ref.shape[0]
    length = bias_ref.shape[0] // 2
    rows = lax.broadcasted_iota(jnp.int32, bias_ref.shape, 0)
    cols = lax.broadcasted_iota(jnp.int32, bias_ref.shape, 1)
    last = jnp.where(rows < length, length, cols + (length + group * tokens))
    bound.wait()
    lowest = jnp.where(lax.axis_index("inner") == 0, length, length - reach_ref[...])
    visible = jnp.logical_and(rows >= lowest, rows <= last)
    bias_ref[...] = jnp.where(visible, 0.0, NEG_FILL).astype(jnp.bfloat16)


def attend_kernel(remote, *refs):
    if remote:
        bias_ref, q_ref, g_ref, own_ref, prev_ref, _, dq_hbm, next_ref, term_ref, dq_ref, sem = refs
    else:
        reach_hbm, q_ref, g_ref, own_ref, prev_ref, _ = refs[:6]
        dq_hbm, next_ref, term_ref, bias_ref, dq_ref, sem, load_sem, reach_ref = refs[6:]
        fetch(reach_hbm, reach_ref, bias_ref, q_ref, load_sem)
    tokens = q_ref.shape[0]
    length = own_ref.shape[0] // 2
    heads = own_ref.shape[1] // HEAD_SIZE
    wide = GROUP * HEAD_SIZE
    span = PAIR * HEAD_SIZE
    group = lax.axis_index("head")
    base = (1 - group if remote else group) * (heads * wide)
    bias = bias_ref[...]
    ident = (
        lax.broadcasted_iota(jnp.int32, (tokens, tokens), 0)
        == lax.broadcasted_iota(jnp.int32, (tokens, tokens), 1)
    )
    ident = jnp.where(ident, 1.0, 0.0).astype(jnp.bfloat16)
    ident = jnp.concatenate([ident] * PAIR, axis=0)

    def column(head):
        return pl.ds(pl.multiple_of(base + head * HEAD_SIZE, HEAD_SIZE), HEAD_SIZE)

    def stacked(ref, step):
        return jnp.concatenate(
            [ref[:, column(h)] for h in range(step * PAIR, (step + 1) * PAIR)], axis=0
        )

    def keys_of(kv):
        at = slice(kv * HEAD_SIZE, (kv + 1) * HEAD_SIZE)
        return jnp.concatenate([prev_ref[:length, at], own_ref[:length, at]], axis=0)

    def values_of(kv):
        at = slice(kv * HEAD_SIZE, (kv + 1) * HEAD_SIZE)
        return jnp.concatenate([prev_ref[length:, at], own_ref[length:, at]], axis=0)

    def project(step):
        kv = step * PAIR // GROUP
        masked_keys = jnp.concatenate([keys_of(kv), bias], axis=1)
        scores = nt(masked_keys, jnp.concatenate([stacked(q_ref, step), ident], axis=1))
        return scores, nt(values_of(kv), stacked(g_ref, step))

    def soften(scores, dprob):
        peak = jnp.max(scores, axis=0, keepdims=True)
        weights = jnp.exp2((scores - peak) * (FACTOR * LOG2_E))
        inverse = 1.0 / jnp.sum(weights, axis=0, keepdims=True)
        row_dot = jnp.sum(weights * dprob, axis=0, keepdims=True) * inverse
        probs = weights * inverse
        dscore = (probs * (dprob - row_dot)).astype(jnp.bfloat16)
        return probs.astype(jnp.bfloat16), dscore

    def finish(step, dscore):
        kv = step * PAIR // GROUP
        dq = (nn(keys_of(kv).T, dscore) * FACTOR).astype(jnp.bfloat16).T
        for i in range(PAIR):
            h = step * PAIR + i
            dq_ref[:, h * HEAD_SIZE : (h + 1) * HEAD_SIZE] = dq[i * tokens : (i + 1) * tokens]

    def send(kv):
        at = slice(kv * wide, (kv + 1) * wide)
        to = pl.ds(pl.multiple_of(base + kv * wide, HEAD_SIZE), wide)
        return pltpu.make_async_copy(dq_ref.at[:, at], dq_hbm.at[:, to], sem.at[kv])

    def gather(step, probs, dscore):
        return nn(dscore, stacked(q_ref, step)), nn(probs, stacked(g_ref, step))

    def deliver(kv, dk, dv):
        dk = dk * FACTOR
        at = slice(kv * HEAD_SIZE, (kv + 1) * HEAD_SIZE)
        next_ref[:length, at] = dk[:length].astype(next_ref.dtype)
        next_ref[length:, at] = dv[:length].astype(next_ref.dtype)
        term_ref[:length, at] = dk[length:].astype(term_ref.dtype)
        term_ref[length:, at] = dv[length:].astype(term_ref.dtype)

    steps = heads * GROUP // PAIR
    per = GROUP // PAIR
    raw = project(0)
    sums = [[0.0, 0.0] for _ in range(heads)]
    for step in range(steps):
        ahead = project(step + 1) if step + 1 < steps else None
        probs, dscore = soften(*raw)
        raw = ahead
        finish(step, dscore)
        kv = step // per
        parts = gather(step, probs, dscore)
        sums[kv] = [x + y for x, y in zip(sums[kv], parts)]
        if (step + 1) % per == 0:
            send(kv).start()
            deliver(kv, *sums[kv])
    for kv in range(heads):
        send(kv).wait()


def attend(own, prev, loads, held, ready, name):
    remote = held is not None
    rows, half = own.shape
    heads = half // HEAD_SIZE
    vmem = pl.BlockSpec(memory_space=pltpu.VMEM)
    anywhere = pl.BlockSpec(memory_space=pl.ANY)
    lanes = heads * GROUP * HEAD_SIZE
    kept = [pinned(x, pltpu.VMEM) for x in (own, prev)]
    if remote:
        dq, bias, query, dout = held
        tokens, width = query.shape
        operands = [pinned(x, pltpu.VMEM) for x in (bias, query, dout)] + kept + [dq]
        in_specs = [vmem] * 5 + [anywhere]
        more_shapes, more_specs, more_scratch = (), [], []
    else:
        tokens, width = loads[1].shape
        operands = [loads[0]] + [pinned(x, pltpu.VMEM) for x in loads[1:]] + kept + [ready]
        in_specs = [anywhere] + [vmem] * 4 + [anywhere]
        more_shapes = (
            in_vmem((rows, tokens), jnp.bfloat16),
        )
        more_specs = [vmem]
        more_scratch = [pltpu.SemaphoreType.DMA((1,)), pltpu.VMEM((1, 1), jnp.int32)]
    return pl.pallas_call(
        functools.partial(attend_kernel, remote),
        out_shape=(
            jax.ShapeDtypeStruct((tokens, width), jnp.bfloat16),
            in_vmem((rows, half), jnp.bfloat16),
            in_vmem((rows, half), jnp.bfloat16 if remote else jnp.float32),
        )
        + more_shapes,
        in_specs=in_specs,
        out_specs=[anywhere, vmem, vmem] + more_specs,
        scratch_shapes=[
            pltpu.VMEM((tokens, lanes), jnp.bfloat16),
            pltpu.SemaphoreType.DMA((heads,)),
        ]
        + more_scratch,
        input_output_aliases={5: 0} if remote else {},
        cost_estimate=pl.CostEstimate(
            flops=10 * heads * GROUP * tokens * rows * HEAD_SIZE,
            bytes_accessed=4 * 1024 * 1024,
            transcendentals=heads * GROUP * tokens * rows,
        ),
        compiler_params=pltpu.CompilerParams(vmem_limit_bytes=32 * 1024 * 1024),
        name=name,
    )(*operands)


def on_device(query, dout, key_mant, value_mantissas, key_exps, value_exponents, reach):
    inner = lax.axis_size("inner")
    length = key_mant.shape[2]
    own = pack(key_mant[0, 0], value_mantissas[0, 0], key_exps[0, 0], value_exponents[0, 0])

    def forward(value):
        return lax.ppermute(value, "inner", [(i, i + 1) for i in range(inner - 1)])

    def backward(value):
        return lax.ppermute(value, "inner", [(i + 1, i) for i in range(inner - 1)])

    def swap(value):
        return lax.ppermute(value, "head", [(0, 1), (1, 0)])

    def across(value, step):
        pairs = [
            (head * inner + at, (1 - head) * inner + at + step)
            for head in range(2)
            for at in range(max(0, -step), min(inner, inner - step))
        ]
        return lax.ppermute(value, ("head", "inner"), pairs)

    prev = forward(own)
    other_own = swap(own)
    other_prev = across(own, 1)
    loads = (reach, pinned(query[0, 0], pltpu.VMEM), pinned(dout[0, 0], pltpu.VMEM))
    dq, next_here, term_here, *held = attend(
        own, prev, loads, None, other_own, "attend_local"
    )
    returned = backward(next_here)
    dq, next_there, term_there = attend(
        other_own, other_prev, None, (dq, *held, *loads[1:]), None, "attend_remote"
    )
    swapped = swap(term_there)
    crossed = across(next_there, -1)
    total = term_here
    for part in (returned, swapped, crossed):
        total = total + part.astype(jnp.float32)
    total = total.astype(jnp.bfloat16)
    return dq[None, None], total[None, None, :length], total[None, None, length:]


def solution(mesh):
    placed = (
        P("outer", "inner", "head", None),
        P("outer", "inner", "head", None),
        P("outer", "inner", None, "head"),
        P("outer", "inner", None, "head"),
        P("outer", "inner", None, "head"),
        P("outer", "inner", None, "head"),
        P("outer", "inner"),
    )
    return jax.shard_map(
        on_device,
        mesh=mesh,
        in_specs=placed,
        out_specs=(
            P("outer", "inner", "head", None),
            P("outer", "inner", None, "head"),
            P("outer", "inner", None, "head"),
        ),
        check_vma=False,
    )
```

```python
import functools

import jax
import jax.numpy as jnp
from jax import lax
from jax.experimental import pallas as pl
from jax.experimental.pallas import tpu as pltpu
from jax.sharding import PartitionSpec as P

QUERY_HEADS = 32
KEY_VALUE_HEADS = 4
HEAD_SIZE = 128
ROWS_PER_SCALE = 128
GROUP = QUERY_HEADS // KEY_VALUE_HEADS
FACTOR = HEAD_SIZE**-0.5
LOG2_E = 1.4426950408889634
NEG_FILL = -1e30
PAIR = 8
PACK_FLOPS = 8 * 10**9
PACK_VMEM = 48


def nt(a, b):
    return lax.dot_general(a, b, (((1,), (1,)), ((), ())), preferred_element_type=jnp.float32)


def nn(a, b):
    return lax.dot_general(a, b, (((1,), (0,)), ((), ())), preferred_element_type=jnp.float32)


def in_vmem(shape, dtype):
    return pltpu.VMEM(shape, dtype)


def pinned(value, space):
    return pltpu.with_memory_space_constraint(value, space)


def pack_kernel(
    key_exps_hbm, value_exps_hbm, key_hbm, value_hbm, out_ref, key_ref, value_ref, key_exps, value_exps, sem
):
    length = key_ref.shape[0]
    loads = [
        pltpu.make_async_copy(key_hbm, key_ref, sem.at[0]),
        pltpu.make_async_copy(value_hbm, value_ref, sem.at[1]),
        pltpu.make_async_copy(key_exps_hbm, key_exps, sem.at[2]),
        pltpu.make_async_copy(value_exps_hbm, value_exps, sem.at[3]),
    ]
    for load in loads:
        load.start()
    for load in loads[2:]:
        load.wait()
    for load, source, exps, base in (
        (loads[0], key_ref, key_exps, 0),
        (loads[1], value_ref, value_exps, length),
    ):
        load.wait()
        for run in range(length // ROWS_PER_SCALE):
            part = slice(run * ROWS_PER_SCALE, (run + 1) * ROWS_PER_SCALE)
            to = slice(base + part.start, base + part.stop)
            for head in range(source.shape[1] // HEAD_SIZE):
                at = slice(head * HEAD_SIZE, (head + 1) * HEAD_SIZE)
                exponent = jnp.full((8, HEAD_SIZE), exps[run, head], jnp.int32).astype(jnp.float32)
                scale = jnp.exp2(exponent)[:1].astype(jnp.bfloat16)
                out_ref[to, at] = source[part, at] * scale


def pack(key_mant, value_mant, key_exps, value_exps):
    length, width = key_mant.shape
    vmem = pl.BlockSpec(memory_space=pltpu.VMEM)
    hbm = pl.BlockSpec(memory_space=pltpu.HBM)
    return pl.pallas_call(
        pack_kernel,
        out_shape=in_vmem((2 * length, width), jnp.bfloat16),
        in_specs=[hbm] * 4,
        out_specs=vmem,
        scratch_shapes=[
            pltpu.VMEM((length, width), jnp.bfloat16),
            pltpu.VMEM((length, width), jnp.bfloat16),
            pltpu.SMEM(key_exps.shape, jnp.int32),
            pltpu.SMEM(value_exps.shape, jnp.int32),
            pltpu.SemaphoreType.DMA((4,)),
        ],
        cost_estimate=pl.CostEstimate(flops=PACK_FLOPS, bytes_accessed=1024 * 1024, transcendentals=0),
        compiler_params=pltpu.CompilerParams(vmem_limit_bytes=PACK_VMEM * 1024 * 1024),
        name="pack",
    )(*(pinned(x, pltpu.HBM) for x in (key_exps, value_exps, key_mant, value_mant)))


def fetch(reach_hbm, reach_ref, bias_ref, q_ref, sem):
    group = lax.axis_index("head")
    bound = pltpu.make_async_copy(reach_hbm, reach_ref, sem.at[0])
    bound.start()
    tokens = q_ref.shape[0]
    length = bias_ref.shape[0] // 2
    rows = lax.broadcasted_iota(jnp.int32, bias_ref.shape, 0)
    cols = lax.broadcasted_iota(jnp.int32, bias_ref.shape, 1)
    last = jnp.where(rows < length, length, cols + (length + group * tokens))
    bound.wait()
    lowest = jnp.where(lax.axis_index("inner") == 0, length, length - reach_ref[...])
    visible = jnp.logical_and(rows >= lowest, rows <= last)
    bias_ref[...] = jnp.where(visible, 0.0, NEG_FILL).astype(jnp.bfloat16)


def columns(group, head):
    return pl.ds(pl.multiple_of((group * 2 * GROUP + head) * HEAD_SIZE, HEAD_SIZE), HEAD_SIZE)


def stacked(ref, group, kv):
    heads = range(kv * GROUP, (kv + 1) * GROUP)
    return jnp.concatenate([ref[:, columns(group, h)] for h in heads], axis=0)


def identity(tokens):
    down = lax.broadcasted_iota(jnp.int32, (tokens, tokens), 0)
    along = lax.broadcasted_iota(jnp.int32, (tokens, tokens), 1)
    one = jnp.where(down == along, 1.0, 0.0).astype(jnp.bfloat16)
    return jnp.concatenate([one] * GROUP, axis=0)


def project(keys, values, bias, queries, grads, ident):
    keys = jnp.concatenate([keys, bias], axis=1)
    scores = nt(keys, jnp.concatenate([queries, ident], axis=1))
    return scores, nt(values, grads)


def weigh(scores, peak):
    return jnp.exp2((scores - peak) * (FACTOR * LOG2_E))


def down(value):
    return jnp.sum(value, axis=0, keepdims=True)


def query_grad(dq_ref, keys, dscore, kv):
    tokens = dq_ref.shape[0]
    dq = (nn(keys.T, dscore) * FACTOR).astype(jnp.bfloat16).T
    for i in range(GROUP):
        head = kv * GROUP + i
        dq_ref[:, head * HEAD_SIZE : (head + 1) * HEAD_SIZE] = dq[i * tokens : (i + 1) * tokens]


def sender(group, dq_ref, dq_hbm, sem):
    wide = GROUP * HEAD_SIZE

    def send(kv):
        at = slice(kv * wide, (kv + 1) * wide)
        to = pl.ds(pl.multiple_of((group * 2 + kv) * wide, wide), wide)
        return pltpu.make_async_copy(dq_ref.at[:, at], dq_hbm.at[:, to], sem.at[kv])

    return send


def local_kernel(
    reach_hbm, q_ref, g_ref, own_ref, prev_ref, other_ref,
    dq_hbm, next_ref, term_ref, bias_ref, w_ref, d_ref, stat_ref,
    dq_ref, sem, load_sem, reach_ref,
):
    fetch(reach_hbm, reach_ref, bias_ref, q_ref, load_sem)
    tokens = q_ref.shape[0]
    length = own_ref.shape[0] // 2
    heads = own_ref.shape[1] // HEAD_SIZE
    group = lax.axis_index("head")
    bias = bias_ref[...]
    ident = identity(tokens)
    send = sender(group, dq_ref, dq_hbm, sem)

    def both(top, kv):
        at = slice(kv * HEAD_SIZE, (kv + 1) * HEAD_SIZE)
        part = slice(top, top + length)
        return jnp.concatenate([prev_ref[part, at], own_ref[part, at]], axis=0)

    def start(kv):
        return project(
            both(0, kv), both(length, kv), bias,
            stacked(q_ref, group, kv), stacked(g_ref, group, kv), ident,
        )

    def start_other(kv):
        at = slice(kv * HEAD_SIZE, (kv + 1) * HEAD_SIZE)
        return project(
            other_ref[:length, at], other_ref[length:, at], bias[length:],
            stacked(q_ref, 1 - group, kv), stacked(g_ref, 1 - group, kv), ident,
        )

    raw = start(0)
    for kv in range(heads):
        scores, dprob = raw
        raw = start(kv + 1) if kv + 1 < heads else start_other(0)
        weights = weigh(scores, jnp.max(scores, axis=0, keepdims=True))
        inverse = 1.0 / down(weights)
        row_dot = down(weights * dprob) * inverse
        probs = weights * inverse
        dscore = (probs * (dprob - row_dot)).astype(jnp.bfloat16)
        probs = probs.astype(jnp.bfloat16)
        query_grad(dq_ref, both(0, kv), dscore, kv)
        send(kv).start()
        dk = nn(dscore, stacked(q_ref, group, kv)) * FACTOR
        dv = nn(probs, stacked(g_ref, group, kv))
        at = slice(kv * HEAD_SIZE, (kv + 1) * HEAD_SIZE)
        next_ref[:length, at] = dk[:length].astype(next_ref.dtype)
        next_ref[length:, at] = dv[:length].astype(next_ref.dtype)
        term_ref[:length, at] = dk[length:]
        term_ref[length:, at] = dv[length:]
    for kv in range(heads):
        scores, dprob = raw
        raw = start_other(kv + 1) if kv + 1 < heads else None
        peak = jnp.max(scores, axis=0, keepdims=True)
        weights = weigh(scores, peak)
        at = slice(kv * GROUP * HEAD_SIZE, (kv + 1) * GROUP * HEAD_SIZE)
        w_ref[:, at] = weights
        d_ref[:, at] = dprob
        stat_ref[0:1, at] = peak
        stat_ref[1:2, at] = down(weights)
        stat_ref[2:3, at] = down(weights * dprob)
    for kv in range(heads):
        send(kv).wait()


def remote_kernel(bias_ref, q_ref, g_ref, prev_ref, w_ref, d_ref, stat_ref, next_ref, term_ref, z_ref):
    tokens = q_ref.shape[0]
    length = prev_ref.shape[0] // 2
    heads = prev_ref.shape[1] // HEAD_SIZE
    group = 1 - lax.axis_index("head")
    bias = bias_ref[:length]
    ident = identity(tokens)

    def start(kv):
        at = slice(kv * HEAD_SIZE, (kv + 1) * HEAD_SIZE)
        return project(
            prev_ref[:length, at], prev_ref[length:, at], bias,
            stacked(q_ref, group, kv), stacked(g_ref, group, kv), ident,
        )

    raw = start(0)
    for kv in range(heads):
        scores, dprob = raw
        raw = start(kv + 1) if kv + 1 < heads else None
        wide = slice(kv * GROUP * HEAD_SIZE, (kv + 1) * GROUP * HEAD_SIZE)
        before = stat_ref[0:1, wide]
        peak = jnp.maximum(jnp.max(scores, axis=0, keepdims=True), before)
        shrink = weigh(before, peak)
        weights = weigh(scores, peak)
        inverse = 1.0 / (down(weights) + shrink * stat_ref[1:2, wide])
        row_dot = (down(weights * dprob) + shrink * stat_ref[2:3, wide]) * inverse
        queries, grads = stacked(q_ref, group, kv), stacked(g_ref, group, kv)
        at = slice(kv * HEAD_SIZE, (kv + 1) * HEAD_SIZE)
        for ref, top, part, scale, grad in (
            (next_ref, 0, weights, inverse, dprob),
            (term_ref, length, w_ref[:, wide], shrink * inverse, d_ref[:, wide]),
        ):
            probs = part * scale
            dscore = (probs * (grad - row_dot)).astype(jnp.bfloat16)
            z_ref[top : top + length, wide] = dscore
            ref[:length, at] = (nn(dscore, queries) * FACTOR).astype(ref.dtype)
            ref[length:, at] = nn(probs.astype(jnp.bfloat16), grads).astype(ref.dtype)


def last_kernel(z_ref, own_ref, prev_ref, _, dq_hbm, dq_ref, sem):
    length = own_ref.shape[0] // 2
    heads = own_ref.shape[1] // HEAD_SIZE
    send = sender(1 - lax.axis_index("head"), dq_ref, dq_hbm, sem)
    for kv in range(heads):
        at = slice(kv * HEAD_SIZE, (kv + 1) * HEAD_SIZE)
        wide = slice(kv * GROUP * HEAD_SIZE, (kv + 1) * GROUP * HEAD_SIZE)
        keys = jnp.concatenate([prev_ref[:length, at], own_ref[:length, at]], axis=0)
        query_grad(dq_ref, keys, z_ref[:, wide], kv)
        send(kv).start()
    for kv in range(heads):
        send(kv).wait()


def call(kernel, operands, spaces, outs, scratch, flops, name, aliases=None):
    specs = {
        pltpu.VMEM: pl.BlockSpec(memory_space=pltpu.VMEM),
        pl.ANY: pl.BlockSpec(memory_space=pl.ANY),
    }
    return pl.pallas_call(
        kernel,
        out_shape=tuple(
            in_vmem(shape, dtype) if space is pltpu.VMEM else jax.ShapeDtypeStruct(shape, dtype)
            for space, shape, dtype in outs
        ),
        in_specs=[specs[space] for space in spaces],
        out_specs=tuple(specs[space] for space, _, _ in outs),
        scratch_shapes=scratch,
        input_output_aliases=aliases or {},
        cost_estimate=pl.CostEstimate(flops=flops, bytes_accessed=4 * 1024 * 1024, transcendentals=0),
        compiler_params=pltpu.CompilerParams(vmem_limit_bytes=32 * 1024 * 1024),
        name=name,
    )(*(pinned(x, space) if space is pltpu.VMEM else x for x, space in zip(operands, spaces)))


def on_device(query, dout, key_mant, value_mantissas, key_exps, value_exponents, reach):
    inner = lax.axis_size("inner")
    length = key_mant.shape[2]
    own = pack(key_mant[0, 0], value_mantissas[0, 0], key_exps[0, 0], value_exponents[0, 0])

    def forward(value):
        return lax.ppermute(value, "inner", [(i, i + 1) for i in range(inner - 1)])

    def backward(value):
        return lax.ppermute(value, "inner", [(i + 1, i) for i in range(inner - 1)])

    def swap(value):
        return lax.ppermute(value, "head", [(0, 1), (1, 0)])

    def across(value, step):
        pairs = [
            (head * inner + at, (1 - head) * inner + at + step)
            for head in range(2)
            for at in range(max(0, -step), min(inner, inner - step))
        ]
        return lax.ppermute(value, ("head", "inner"), pairs)

    prev = forward(own)
    other_own = swap(own)
    other_prev = across(own, 1)
    loads = (reach, pinned(query[0, 0], pltpu.VMEM), pinned(dout[0, 0], pltpu.VMEM))
    reach, query, dout = loads
    rows, half = own.shape
    tokens, width = query.shape
    lanes = width // 2
    fast, anywhere, bf16, f32 = pltpu.VMEM, pl.ANY, jnp.bfloat16, jnp.float32
    flops = 12 * lanes * rows * HEAD_SIZE
    stage = [pltpu.VMEM((tokens, lanes), bf16), pltpu.SemaphoreType.DMA((2,))]
    dq, next_here, term_here, bias, weights, dprob, stats = call(
        local_kernel,
        (reach, query, dout, own, prev, other_own),
        (anywhere, fast, fast, fast, fast, fast),
        (
            (anywhere, (tokens, width), bf16),
            (fast, (rows, half), bf16),
            (fast, (rows, half), f32),
            (fast, (rows, tokens), bf16),
            (fast, (length, lanes), f32),
            (fast, (length, lanes), f32),
            (fast, (8, lanes), f32),
        ),
        stage + [pltpu.SemaphoreType.DMA((1,)), pltpu.VMEM((1, 1), jnp.int32)],
        flops,
        "local",
    )
    returned = backward(next_here)
    next_there, term_there, dscore = call(
        remote_kernel,
        (bias, query, dout, other_prev, weights, dprob, stats),
        (fast,) * 7,
        ((fast, (rows, half), bf16), (fast, (rows, half), bf16), (fast, (rows, lanes), bf16)),
        [],
        flops,
        "remote",
    )
    swapped = swap(term_there)
    crossed = across(next_there, -1)
    (dq,) = call(
        last_kernel,
        (dscore, other_own, other_prev, dq),
        (fast, fast, fast, anywhere),
        ((anywhere, (tokens, width), bf16),),
        stage,
        flops,
        "last",
        {3: 0},
    )
    total = term_here
    for part in (returned, swapped, crossed):
        total = total + part.astype(jnp.float32)
    total = total.astype(jnp.bfloat16)
    return dq[None, None], total[None, None, :length], total[None, None, length:]


def solution(mesh):
    placed = (
        P("outer", "inner", "head", None),
        P("outer", "inner", "head", None),
        P("outer", "inner", None, "head"),
        P("outer", "inner", None, "head"),
        P("outer", "inner", None, "head"),
        P("outer", "inner", None, "head"),
        P("outer", "inner"),
    )
    return jax.shard_map(
        on_device,
        mesh=mesh,
        in_specs=placed,
        out_specs=(
            P("outer", "inner", "head", None),
            P("outer", "inner", None, "head"),
            P("outer", "inner", None, "head"),
        ),
        check_vma=False,
    )
```

```python
import functools

import jax
import jax.numpy as jnp
from jax import lax
from jax.experimental import pallas as pl
from jax.experimental.pallas import tpu as pltpu
from jax.sharding import PartitionSpec as P

QUERY_HEADS = 32
KEY_VALUE_HEADS = 4
HEAD_SIZE = 128
ROWS_PER_SCALE = 128
GROUP = QUERY_HEADS // KEY_VALUE_HEADS
FACTOR = HEAD_SIZE**-0.5
LOG2_E = 1.4426950408889634
NEG_FILL = -1e30
PAIR = 8
PACK_FLOPS = 8 * 10**9
PACK_VMEM = 48


def nt(a, b):
    return lax.dot_general(a, b, (((1,), (1,)), ((), ())), preferred_element_type=jnp.float32)


def nn(a, b):
    return lax.dot_general(a, b, (((1,), (0,)), ((), ())), preferred_element_type=jnp.float32)


def in_vmem(shape, dtype):
    return pltpu.VMEM(shape, dtype)


def pinned(value, space):
    return pltpu.with_memory_space_constraint(value, space)


def pack_kernel(
    key_exps_hbm, value_exps_hbm, key_hbm, value_hbm, out_ref, key_ref, value_ref, key_exps, value_exps, sem
):
    length = key_ref.shape[0]
    loads = [
        pltpu.make_async_copy(key_hbm, key_ref, sem.at[0]),
        pltpu.make_async_copy(value_hbm, value_ref, sem.at[1]),
        pltpu.make_async_copy(key_exps_hbm, key_exps, sem.at[2]),
        pltpu.make_async_copy(value_exps_hbm, value_exps, sem.at[3]),
    ]
    for load in loads:
        load.start()
    for load in loads[2:]:
        load.wait()
    for load, source, exps, base in (
        (loads[0], key_ref, key_exps, 0),
        (loads[1], value_ref, value_exps, length),
    ):
        load.wait()
        for run in range(length // ROWS_PER_SCALE):
            part = slice(run * ROWS_PER_SCALE, (run + 1) * ROWS_PER_SCALE)
            to = slice(base + part.start, base + part.stop)
            for head in range(source.shape[1] // HEAD_SIZE):
                at = slice(head * HEAD_SIZE, (head + 1) * HEAD_SIZE)
                exponent = jnp.full((8, HEAD_SIZE), exps[run, head], jnp.int32).astype(jnp.float32)
                scale = jnp.exp2(exponent)[:1].astype(jnp.bfloat16)
                out_ref[to, at] = source[part, at] * scale


def pack(key_mant, value_mant, key_exps, value_exps):
    length, width = key_mant.shape
    vmem = pl.BlockSpec(memory_space=pltpu.VMEM)
    hbm = pl.BlockSpec(memory_space=pltpu.HBM)
    return pl.pallas_call(
        pack_kernel,
        out_shape=in_vmem((2 * length, width), jnp.bfloat16),
        in_specs=[hbm] * 4,
        out_specs=vmem,
        scratch_shapes=[
            pltpu.VMEM((length, width), jnp.bfloat16),
            pltpu.VMEM((length, width), jnp.bfloat16),
            pltpu.SMEM(key_exps.shape, jnp.int32),
            pltpu.SMEM(value_exps.shape, jnp.int32),
            pltpu.SemaphoreType.DMA((4,)),
        ],
        cost_estimate=pl.CostEstimate(flops=PACK_FLOPS, bytes_accessed=1024 * 1024, transcendentals=0),
        compiler_params=pltpu.CompilerParams(vmem_limit_bytes=PACK_VMEM * 1024 * 1024),
        name="pack",
    )(*(pinned(x, pltpu.HBM) for x in (key_exps, value_exps, key_mant, value_mant)))


def fetch(reach_hbm, reach_ref, bias_ref, q_ref, sem):
    group = lax.axis_index("head")
    bound = pltpu.make_async_copy(reach_hbm, reach_ref, sem.at[0])
    bound.start()
    tokens = q_ref.shape[0]
    length = bias_ref.shape[0] // 2
    rows = lax.broadcasted_iota(jnp.int32, bias_ref.shape, 0)
    cols = lax.broadcasted_iota(jnp.int32, bias_ref.shape, 1)
    last = jnp.where(rows < length, length, cols + (length + group * tokens))
    bound.wait()
    lowest = jnp.where(lax.axis_index("inner") == 0, length, length - reach_ref[...])
    visible = jnp.logical_and(rows >= lowest, rows <= last)
    bias_ref[...] = jnp.where(visible, 0.0, NEG_FILL).astype(jnp.bfloat16)


def columns(group, head):
    return pl.ds(pl.multiple_of((group * 2 * GROUP + head) * HEAD_SIZE, HEAD_SIZE), HEAD_SIZE)


def stacked(ref, group, kv):
    heads = range(kv * GROUP, (kv + 1) * GROUP)
    return jnp.concatenate([ref[:, columns(group, h)] for h in heads], axis=0)


def identity(tokens):
    down = lax.broadcasted_iota(jnp.int32, (tokens, tokens), 0)
    along = lax.broadcasted_iota(jnp.int32, (tokens, tokens), 1)
    one = jnp.where(down == along, 1.0, 0.0).astype(jnp.bfloat16)
    return jnp.concatenate([one] * GROUP, axis=0)


def project(keys, values, bias, queries, grads, ident):
    keys = jnp.concatenate([keys, bias], axis=1)
    scores = nt(keys, jnp.concatenate([queries, ident], axis=1))
    return scores, nt(values, grads)


def weigh(scores, peak):
    return jnp.exp2((scores - peak) * (FACTOR * LOG2_E))


def down(value):
    return jnp.sum(value, axis=0, keepdims=True)


def query_grad(dq_ref, keys, dscore, kv):
    tokens = dq_ref.shape[0]
    dq = (nn(keys.T, dscore) * FACTOR).astype(jnp.bfloat16).T
    for i in range(GROUP):
        head = kv * GROUP + i
        dq_ref[:, head * HEAD_SIZE : (head + 1) * HEAD_SIZE] = dq[i * tokens : (i + 1) * tokens]


def sender(group, dq_ref, dq_hbm, sem):
    wide = GROUP * HEAD_SIZE

    def send(kv):
        at = slice(kv * wide, (kv + 1) * wide)
        to = pl.ds(pl.multiple_of((group * 2 + kv) * wide, wide), wide)
        return pltpu.make_async_copy(dq_ref.at[:, at], dq_hbm.at[:, to], sem.at[kv])

    return send


def local_kernel(
    reach_hbm, q_ref, g_ref, own_ref, prev_ref,
    dq_hbm, next_ref, term_ref, bias_ref,
    dq_ref, sem, load_sem, reach_ref,
):
    fetch(reach_hbm, reach_ref, bias_ref, q_ref, load_sem)
    tokens = q_ref.shape[0]
    length = own_ref.shape[0] // 2
    heads = own_ref.shape[1] // HEAD_SIZE
    group = lax.axis_index("head")
    bias = bias_ref[...]
    ident = identity(tokens)
    send = sender(group, dq_ref, dq_hbm, sem)

    def both(top, kv):
        at = slice(kv * HEAD_SIZE, (kv + 1) * HEAD_SIZE)
        part = slice(top, top + length)
        return jnp.concatenate([prev_ref[part, at], own_ref[part, at]], axis=0)

    def start(kv):
        return project(
            both(0, kv), both(length, kv), bias,
            stacked(q_ref, group, kv), stacked(g_ref, group, kv), ident,
        )

    raw = start(0)
    for kv in range(heads):
        scores, dprob = raw
        raw = start(kv + 1) if kv + 1 < heads else None
        weights = weigh(scores, jnp.max(scores, axis=0, keepdims=True))
        inverse = 1.0 / down(weights)
        row_dot = down(weights * dprob) * inverse
        probs = weights * inverse
        dscore = (probs * (dprob - row_dot)).astype(jnp.bfloat16)
        probs = probs.astype(jnp.bfloat16)
        query_grad(dq_ref, both(0, kv), dscore, kv)
        send(kv).start()
        dk = nn(dscore, stacked(q_ref, group, kv)) * FACTOR
        dv = nn(probs, stacked(g_ref, group, kv))
        at = slice(kv * HEAD_SIZE, (kv + 1) * HEAD_SIZE)
        next_ref[:length, at] = dk[:length].astype(next_ref.dtype)
        next_ref[length:, at] = dv[:length].astype(next_ref.dtype)
        term_ref[:length, at] = dk[length:]
        term_ref[length:, at] = dv[length:]
    for kv in range(heads):
        send(kv).wait()


def partial_kernel(bias_ref, q_ref, g_ref, other_ref, w_ref, d_ref, stat_ref):
    tokens = q_ref.shape[0]
    length = other_ref.shape[0] // 2
    heads = other_ref.shape[1] // HEAD_SIZE
    group = 1 - lax.axis_index("head")
    bias = bias_ref[length:]
    ident = identity(tokens)

    def start(kv):
        at = slice(kv * HEAD_SIZE, (kv + 1) * HEAD_SIZE)
        return project(
            other_ref[:length, at], other_ref[length:, at], bias,
            stacked(q_ref, group, kv), stacked(g_ref, group, kv), ident,
        )

    raw = start(0)
    for kv in range(heads):
        scores, dprob = raw
        raw = start(kv + 1) if kv + 1 < heads else None
        peak = jnp.max(scores, axis=0, keepdims=True)
        weights = weigh(scores, peak)
        at = slice(kv * GROUP * HEAD_SIZE, (kv + 1) * GROUP * HEAD_SIZE)
        w_ref[:, at] = weights
        d_ref[:, at] = dprob
        stat_ref[0:1, at] = peak
        stat_ref[1:2, at] = down(weights)
        stat_ref[2:3, at] = down(weights * dprob)


def remote_kernel(bias_ref, q_ref, g_ref, prev_ref, w_ref, d_ref, stat_ref, next_ref, term_ref, z_ref):
    tokens = q_ref.shape[0]
    length = prev_ref.shape[0] // 2
    heads = prev_ref.shape[1] // HEAD_SIZE
    group = 1 - lax.axis_index("head")
    bias = bias_ref[:length]
    ident = identity(tokens)

    def start(kv):
        at = slice(kv * HEAD_SIZE, (kv + 1) * HEAD_SIZE)
        return project(
            prev_ref[:length, at], prev_ref[length:, at], bias,
            stacked(q_ref, group, kv), stacked(g_ref, group, kv), ident,
        )

    raw = start(0)
    for kv in range(heads):
        scores, dprob = raw
        raw = start(kv + 1) if kv + 1 < heads else None
        wide = slice(kv * GROUP * HEAD_SIZE, (kv + 1) * GROUP * HEAD_SIZE)
        before = stat_ref[0:1, wide]
        peak = jnp.maximum(jnp.max(scores, axis=0, keepdims=True), before)
        shrink = weigh(before, peak)
        weights = weigh(scores, peak)
        inverse = 1.0 / (down(weights) + shrink * stat_ref[1:2, wide])
        row_dot = (down(weights * dprob) + shrink * stat_ref[2:3, wide]) * inverse
        queries, grads = stacked(q_ref, group, kv), stacked(g_ref, group, kv)
        at = slice(kv * HEAD_SIZE, (kv + 1) * HEAD_SIZE)
        for ref, top, part, scale, grad in (
            (next_ref, 0, weights, inverse, dprob),
            (term_ref, length, w_ref[:, wide], shrink * inverse, d_ref[:, wide]),
        ):
            probs = part * scale
            dscore = (probs * (grad - row_dot)).astype(jnp.bfloat16)
            z_ref[top : top + length, wide] = dscore
            ref[:length, at] = (nn(dscore, queries) * FACTOR).astype(ref.dtype)
            ref[length:, at] = nn(probs.astype(jnp.bfloat16), grads).astype(ref.dtype)


def last_kernel(z_ref, own_ref, prev_ref, term_ref, back_ref, _, dq_hbm, sum_ref, dq_ref, sem):
    length = own_ref.shape[0] // 2
    heads = own_ref.shape[1] // HEAD_SIZE
    send = sender(1 - lax.axis_index("head"), dq_ref, dq_hbm, sem)
    for kv in range(heads):
        at = slice(kv * HEAD_SIZE, (kv + 1) * HEAD_SIZE)
        wide = slice(kv * GROUP * HEAD_SIZE, (kv + 1) * GROUP * HEAD_SIZE)
        keys = jnp.concatenate([prev_ref[:length, at], own_ref[:length, at]], axis=0)
        query_grad(dq_ref, keys, z_ref[:, wide], kv)
        send(kv).start()
    sum_ref[...] = term_ref[...] + back_ref[...].astype(jnp.float32)
    for kv in range(heads):
        send(kv).wait()


def call(kernel, operands, spaces, outs, scratch, flops, name, aliases=None):
    specs = {
        pltpu.VMEM: pl.BlockSpec(memory_space=pltpu.VMEM),
        pl.ANY: pl.BlockSpec(memory_space=pl.ANY),
    }
    return pl.pallas_call(
        kernel,
        out_shape=tuple(
            in_vmem(shape, dtype) if space is pltpu.VMEM else jax.ShapeDtypeStruct(shape, dtype)
            for space, shape, dtype in outs
        ),
        in_specs=[specs[space] for space in spaces],
        out_specs=tuple(specs[space] for space, _, _ in outs),
        scratch_shapes=scratch,
        input_output_aliases=aliases or {},
        cost_estimate=pl.CostEstimate(flops=flops, bytes_accessed=4 * 1024 * 1024, transcendentals=0),
        compiler_params=pltpu.CompilerParams(vmem_limit_bytes=32 * 1024 * 1024),
        name=name,
    )(*(pinned(x, space) if space is pltpu.VMEM else x for x, space in zip(operands, spaces)))


def on_device(query, dout, key_mant, value_mantissas, key_exps, value_exponents, reach):
    inner = lax.axis_size("inner")
    length = key_mant.shape[2]
    own = pack(key_mant[0, 0], value_mantissas[0, 0], key_exps[0, 0], value_exponents[0, 0])

    def forward(value):
        return lax.ppermute(value, "inner", [(i, i + 1) for i in range(inner - 1)])

    def backward(value):
        return lax.ppermute(value, "inner", [(i + 1, i) for i in range(inner - 1)])

    def swap(value):
        return lax.ppermute(value, "head", [(0, 1), (1, 0)])

    def across(value, step):
        pairs = [
            (head * inner + at, (1 - head) * inner + at + step)
            for head in range(2)
            for at in range(max(0, -step), min(inner, inner - step))
        ]
        return lax.ppermute(value, ("head", "inner"), pairs)

    prev = forward(own)
    other_own = swap(own)
    other_prev = across(own, 1)
    loads = (reach, pinned(query[0, 0], pltpu.VMEM), pinned(dout[0, 0], pltpu.VMEM))
    reach, query, dout = loads
    rows, half = own.shape
    tokens, width = query.shape
    lanes = width // 2
    fast, anywhere, bf16, f32 = pltpu.VMEM, pl.ANY, jnp.bfloat16, jnp.float32
    flops = 12 * lanes * rows * HEAD_SIZE
    stage = [pltpu.VMEM((tokens, lanes), bf16), pltpu.SemaphoreType.DMA((2,))]
    dq, next_here, term_here, bias = call(
        local_kernel,
        (reach, query, dout, own, prev),
        (anywhere, fast, fast, fast, fast),
        (
            (anywhere, (tokens, width), bf16),
            (fast, (rows, half), bf16),
            (fast, (rows, half), f32),
            (fast, (rows, tokens), bf16),
        ),
        stage + [pltpu.SemaphoreType.DMA((1,)), pltpu.VMEM((1, 1), jnp.int32)],
        flops,
        "local",
    )
    returned = backward(next_here)
    weights, dprob, stats = call(
        partial_kernel,
        (bias, query, dout, other_own),
        (fast,) * 4,
        ((fast, (length, lanes), f32), (fast, (length, lanes), f32), (fast, (8, lanes), f32)),
        [],
        flops // 4,
        "partial",
    )
    next_there, term_there, dscore = call(
        remote_kernel,
        (bias, query, dout, other_prev, weights, dprob, stats),
        (fast,) * 7,
        ((fast, (rows, half), bf16), (fast, (rows, half), bf16), (fast, (rows, lanes), bf16)),
        [],
        flops,
        "remote",
    )
    swapped = swap(term_there)
    crossed = across(next_there, -1)
    dq, total = call(
        last_kernel,
        (dscore, other_own, other_prev, term_here, returned, dq),
        (fast, fast, fast, fast, fast, anywhere),
        ((anywhere, (tokens, width), bf16), (fast, (rows, half), f32)),
        stage,
        flops,
        "last",
        {5: 0},
    )
    for part in (crossed, swapped):
        total = total + part.astype(jnp.float32)
    total = total.astype(jnp.bfloat16)
    return dq[None, None], total[None, None, :length], total[None, None, length:]


def solution(mesh):
    placed = (
        P("outer", "inner", "head", None),
        P("outer", "inner", "head", None),
        P("outer", "inner", None, "head"),
        P("outer", "inner", None, "head"),
        P("outer", "inner", None, "head"),
        P("outer", "inner", None, "head"),
        P("outer", "inner"),
    )
    return jax.shard_map(
        on_device,
        mesh=mesh,
        in_specs=placed,
        out_specs=(
            P("outer", "inner", "head", None),
            P("outer", "inner", None, "head"),
            P("outer", "inner", None, "head"),
        ),
        check_vma=False,
    )
```

```python
import functools

import jax
import jax.numpy as jnp
from jax import lax
from jax.experimental import pallas as pl
from jax.experimental.pallas import tpu as pltpu
from jax.sharding import PartitionSpec as P

QUERY_HEADS = 32
KEY_VALUE_HEADS = 4
HEAD_SIZE = 128
ROWS_PER_SCALE = 128
GROUP = QUERY_HEADS // KEY_VALUE_HEADS
FACTOR = HEAD_SIZE**-0.5
LOG2_E = 1.4426950408889634
NEG_FILL = -1e30
PAIR = 8
PACK_FLOPS = 8 * 10**9
PACK_VMEM = 48


def nt(a, b):
    return lax.dot_general(a, b, (((1,), (1,)), ((), ())), preferred_element_type=jnp.float32)


def nn(a, b):
    return lax.dot_general(a, b, (((1,), (0,)), ((), ())), preferred_element_type=jnp.float32)


def in_vmem(shape, dtype):
    return pltpu.VMEM(shape, dtype)


def pinned(value, space):
    return pltpu.with_memory_space_constraint(value, space)


def pack_kernel(
    key_exps_hbm, value_exps_hbm, key_hbm, value_hbm, out_ref, key_ref, value_ref, key_exps, value_exps, sem
):
    length = key_ref.shape[0]
    loads = [
        pltpu.make_async_copy(key_hbm, key_ref, sem.at[0]),
        pltpu.make_async_copy(value_hbm, value_ref, sem.at[1]),
        pltpu.make_async_copy(key_exps_hbm, key_exps, sem.at[2]),
        pltpu.make_async_copy(value_exps_hbm, value_exps, sem.at[3]),
    ]
    for load in loads:
        load.start()
    for load in loads[2:]:
        load.wait()
    for load, source, exps, base in (
        (loads[0], key_ref, key_exps, 0),
        (loads[1], value_ref, value_exps, length),
    ):
        load.wait()
        for run in range(length // ROWS_PER_SCALE):
            part = slice(run * ROWS_PER_SCALE, (run + 1) * ROWS_PER_SCALE)
            to = slice(base + part.start, base + part.stop)
            for head in range(source.shape[1] // HEAD_SIZE):
                at = slice(head * HEAD_SIZE, (head + 1) * HEAD_SIZE)
                exponent = jnp.full((8, HEAD_SIZE), exps[run, head], jnp.int32).astype(jnp.float32)
                scale = jnp.exp2(exponent)[:1].astype(jnp.bfloat16)
                out_ref[to, at] = source[part, at] * scale


def pack(key_mant, value_mant, key_exps, value_exps):
    length, width = key_mant.shape
    vmem = pl.BlockSpec(memory_space=pltpu.VMEM)
    hbm = pl.BlockSpec(memory_space=pltpu.HBM)
    return pl.pallas_call(
        pack_kernel,
        out_shape=in_vmem((2 * length, width), jnp.bfloat16),
        in_specs=[hbm] * 4,
        out_specs=vmem,
        scratch_shapes=[
            pltpu.VMEM((length, width), jnp.bfloat16),
            pltpu.VMEM((length, width), jnp.bfloat16),
            pltpu.SMEM(key_exps.shape, jnp.int32),
            pltpu.SMEM(value_exps.shape, jnp.int32),
            pltpu.SemaphoreType.DMA((4,)),
        ],
        cost_estimate=pl.CostEstimate(flops=PACK_FLOPS, bytes_accessed=1024 * 1024, transcendentals=0),
        compiler_params=pltpu.CompilerParams(vmem_limit_bytes=PACK_VMEM * 1024 * 1024),
        name="pack",
    )(*(pinned(x, pltpu.HBM) for x in (key_exps, value_exps, key_mant, value_mant)))


def fetch(reach_hbm, reach_ref, bias_ref, q_ref, sem):
    group = lax.axis_index("head")
    bound = pltpu.make_async_copy(reach_hbm, reach_ref, sem.at[0])
    bound.start()
    tokens = q_ref.shape[0]
    length = bias_ref.shape[0] // 2
    rows = lax.broadcasted_iota(jnp.int32, bias_ref.shape, 0)
    cols = lax.broadcasted_iota(jnp.int32, bias_ref.shape, 1)
    last = jnp.where(rows < length, length, cols + (length + group * tokens))
    bound.wait()
    lowest = jnp.where(lax.axis_index("inner") == 0, length, length - reach_ref[...])
    visible = jnp.logical_and(rows >= lowest, rows <= last)
    bias_ref[...] = jnp.where(visible, 0.0, NEG_FILL).astype(jnp.bfloat16)


def columns(group, head):
    return pl.ds(pl.multiple_of((group * 2 * GROUP + head) * HEAD_SIZE, HEAD_SIZE), HEAD_SIZE)


def stacked(ref, group, kv):
    heads = range(kv * GROUP, (kv + 1) * GROUP)
    return jnp.concatenate([ref[:, columns(group, h)] for h in heads], axis=0)


def identity(tokens):
    down = lax.broadcasted_iota(jnp.int32, (tokens, tokens), 0)
    along = lax.broadcasted_iota(jnp.int32, (tokens, tokens), 1)
    one = jnp.where(down == along, 1.0, 0.0).astype(jnp.bfloat16)
    return jnp.concatenate([one] * GROUP, axis=0)


def project(keys, values, bias, queries, grads, ident):
    keys = jnp.concatenate([keys, bias], axis=1)
    scores = nt(keys, jnp.concatenate([queries, ident], axis=1))
    return scores, nt(values, grads)


def weigh(scores, peak):
    return jnp.exp2((scores - peak) * (FACTOR * LOG2_E))


def down(value):
    return jnp.sum(value, axis=0, keepdims=True)


def query_grad(dq_ref, keys, dscore, kv):
    tokens = dq_ref.shape[0]
    dq = (nn(keys.T, dscore) * FACTOR).astype(jnp.bfloat16).T
    for i in range(GROUP):
        head = kv * GROUP + i
        dq_ref[:, head * HEAD_SIZE : (head + 1) * HEAD_SIZE] = dq[i * tokens : (i + 1) * tokens]


def sender(group, dq_ref, dq_hbm, sem):
    wide = GROUP * HEAD_SIZE

    def send(kv):
        at = slice(kv * wide, (kv + 1) * wide)
        to = pl.ds(pl.multiple_of((group * 2 + kv) * wide, wide), wide)
        return pltpu.make_async_copy(dq_ref.at[:, at], dq_hbm.at[:, to], sem.at[kv])

    return send


def local_kernel(
    reach_hbm, q_ref, g_ref, own_ref, prev_ref,
    dq_hbm, next_ref, term_ref, bias_ref,
    dq_ref, sem, load_sem, reach_ref,
):
    fetch(reach_hbm, reach_ref, bias_ref, q_ref, load_sem)
    tokens = q_ref.shape[0]
    length = own_ref.shape[0] // 2
    heads = own_ref.shape[1] // HEAD_SIZE
    group = lax.axis_index("head")
    bias = bias_ref[...]
    ident = identity(tokens)
    send = sender(group, dq_ref, dq_hbm, sem)

    def both(top, kv):
        at = slice(kv * HEAD_SIZE, (kv + 1) * HEAD_SIZE)
        part = slice(top, top + length)
        return jnp.concatenate([prev_ref[part, at], own_ref[part, at]], axis=0)

    def start(kv):
        return project(
            both(0, kv), both(length, kv), bias,
            stacked(q_ref, group, kv), stacked(g_ref, group, kv), ident,
        )

    raw = start(0)
    for kv in range(heads):
        scores, dprob = raw
        raw = start(kv + 1) if kv + 1 < heads else None
        weights = weigh(scores, jnp.max(scores, axis=0, keepdims=True))
        inverse = 1.0 / down(weights)
        row_dot = down(weights * dprob) * inverse
        probs = weights * inverse
        dscore = (probs * (dprob - row_dot)).astype(jnp.bfloat16)
        probs = probs.astype(jnp.bfloat16)
        query_grad(dq_ref, both(0, kv), dscore, kv)
        send(kv).start()
        dk = nn(dscore, stacked(q_ref, group, kv)) * FACTOR
        dv = nn(probs, stacked(g_ref, group, kv))
        at = slice(kv * HEAD_SIZE, (kv + 1) * HEAD_SIZE)
        next_ref[:length, at] = dk[:length].astype(next_ref.dtype)
        next_ref[length:, at] = dv[:length].astype(next_ref.dtype)
        term_ref[:length, at] = dk[length:]
        term_ref[length:, at] = dv[length:]
    for kv in range(heads):
        send(kv).wait()


def partial_kernel(bias_ref, q_ref, g_ref, other_ref, w_ref, d_ref, stat_ref):
    tokens = q_ref.shape[0]
    length = other_ref.shape[0] // 2
    heads = other_ref.shape[1] // HEAD_SIZE
    group = 1 - lax.axis_index("head")
    bias = bias_ref[length:]
    ident = identity(tokens)

    def start(kv):
        at = slice(kv * HEAD_SIZE, (kv + 1) * HEAD_SIZE)
        return project(
            other_ref[:length, at], other_ref[length:, at], bias,
            stacked(q_ref, group, kv), stacked(g_ref, group, kv), ident,
        )

    raw = start(0)
    for kv in range(heads):
        scores, dprob = raw
        raw = start(kv + 1) if kv + 1 < heads else None
        peak = jnp.max(scores, axis=0, keepdims=True)
        weights = weigh(scores, peak)
        at = slice(kv * GROUP * HEAD_SIZE, (kv + 1) * GROUP * HEAD_SIZE)
        w_ref[:, at] = weights
        d_ref[:, at] = dprob
        stat_ref[0:1, at] = peak
        stat_ref[1:2, at] = down(weights)
        stat_ref[2:3, at] = down(weights * dprob)


def remote_kernel(bias_ref, q_ref, g_ref, prev_ref, w_ref, d_ref, stat_ref, next_ref, term_ref, z_ref):
    tokens = q_ref.shape[0]
    length = prev_ref.shape[0] // 2
    heads = prev_ref.shape[1] // HEAD_SIZE
    group = 1 - lax.axis_index("head")
    bias = bias_ref[:length]
    ident = identity(tokens)

    def start(kv):
        at = slice(kv * HEAD_SIZE, (kv + 1) * HEAD_SIZE)
        return project(
            prev_ref[:length, at], prev_ref[length:, at], bias,
            stacked(q_ref, group, kv), stacked(g_ref, group, kv), ident,
        )

    raw = start(0)
    for kv in range(heads):
        scores, dprob = raw
        raw = start(kv + 1) if kv + 1 < heads else None
        wide = slice(kv * GROUP * HEAD_SIZE, (kv + 1) * GROUP * HEAD_SIZE)
        before = stat_ref[0:1, wide]
        peak = jnp.maximum(jnp.max(scores, axis=0, keepdims=True), before)
        shrink = weigh(before, peak)
        weights = weigh(scores, peak)
        inverse = 1.0 / (down(weights) + shrink * stat_ref[1:2, wide])
        row_dot = (down(weights * dprob) + shrink * stat_ref[2:3, wide]) * inverse
        queries, grads = stacked(q_ref, group, kv), stacked(g_ref, group, kv)
        at = slice(kv * HEAD_SIZE, (kv + 1) * HEAD_SIZE)
        parts = []
        for part, scale, grad in (
            (weights, inverse, dprob),
            (w_ref[:, wide], shrink * inverse, d_ref[:, wide]),
        ):
            probs = part * scale
            parts.append((probs.astype(jnp.bfloat16), (probs * (grad - row_dot)).astype(jnp.bfloat16)))
        probs, dscore = (jnp.concatenate(pair, axis=0) for pair in zip(*parts))
        z_ref[:, wide] = dscore
        dk, dv = nn(dscore, queries) * FACTOR, nn(probs, grads)
        for ref, rows in ((next_ref, slice(0, length)), (term_ref, slice(length, 2 * length))):
            ref[:length, at] = dk[rows].astype(ref.dtype)
            ref[length:, at] = dv[rows].astype(ref.dtype)


def last_kernel(z_ref, own_ref, prev_ref, term_ref, back_ref, _, dq_hbm, sum_ref, dq_ref, sem):
    length = own_ref.shape[0] // 2
    heads = own_ref.shape[1] // HEAD_SIZE
    send = sender(1 - lax.axis_index("head"), dq_ref, dq_hbm, sem)
    for kv in range(heads):
        at = slice(kv * HEAD_SIZE, (kv + 1) * HEAD_SIZE)
        wide = slice(kv * GROUP * HEAD_SIZE, (kv + 1) * GROUP * HEAD_SIZE)
        keys = jnp.concatenate([prev_ref[:length, at], own_ref[:length, at]], axis=0)
        query_grad(dq_ref, keys, z_ref[:, wide], kv)
        send(kv).start()
    sum_ref[...] = term_ref[...] + back_ref[...].astype(jnp.float32)
    for kv in range(heads):
        send(kv).wait()


def call(kernel, operands, spaces, outs, scratch, flops, name, aliases=None):
    specs = {
        pltpu.VMEM: pl.BlockSpec(memory_space=pltpu.VMEM),
        pl.ANY: pl.BlockSpec(memory_space=pl.ANY),
    }
    return pl.pallas_call(
        kernel,
        out_shape=tuple(
            in_vmem(shape, dtype) if space is pltpu.VMEM else jax.ShapeDtypeStruct(shape, dtype)
            for space, shape, dtype in outs
        ),
        in_specs=[specs[space] for space in spaces],
        out_specs=tuple(specs[space] for space, _, _ in outs),
        scratch_shapes=scratch,
        input_output_aliases=aliases or {},
        cost_estimate=pl.CostEstimate(flops=flops, bytes_accessed=4 * 1024 * 1024, transcendentals=0),
        compiler_params=pltpu.CompilerParams(vmem_limit_bytes=32 * 1024 * 1024),
        name=name,
    )(*(pinned(x, space) if space is pltpu.VMEM else x for x, space in zip(operands, spaces)))


def on_device(query, dout, key_mant, value_mantissas, key_exps, value_exponents, reach):
    inner = lax.axis_size("inner")
    length = key_mant.shape[2]
    own = pack(key_mant[0, 0], value_mantissas[0, 0], key_exps[0, 0], value_exponents[0, 0])

    def forward(value):
        return lax.ppermute(value, "inner", [(i, i + 1) for i in range(inner - 1)])

    def backward(value):
        return lax.ppermute(value, "inner", [(i + 1, i) for i in range(inner - 1)])

    def swap(value):
        return lax.ppermute(value, "head", [(0, 1), (1, 0)])

    def across(value, step):
        pairs = [
            (head * inner + at, (1 - head) * inner + at + step)
            for head in range(2)
            for at in range(max(0, -step), min(inner, inner - step))
        ]
        return lax.ppermute(value, ("head", "inner"), pairs)

    prev = forward(own)
    other_own = swap(own)
    other_prev = across(own, 1)
    loads = (reach, pinned(query[0, 0], pltpu.VMEM), pinned(dout[0, 0], pltpu.VMEM))
    reach, query, dout = loads
    rows, half = own.shape
    tokens, width = query.shape
    lanes = width // 2
    fast, anywhere, bf16, f32 = pltpu.VMEM, pl.ANY, jnp.bfloat16, jnp.float32
    flops = 12 * lanes * rows * HEAD_SIZE
    stage = [pltpu.VMEM((tokens, lanes), bf16), pltpu.SemaphoreType.DMA((2,))]
    dq, next_here, term_here, bias = call(
        local_kernel,
        (reach, query, dout, own, prev),
        (anywhere, fast, fast, fast, fast),
        (
            (anywhere, (tokens, width), bf16),
            (fast, (rows, half), bf16),
            (fast, (rows, half), f32),
            (fast, (rows, tokens), bf16),
        ),
        stage + [pltpu.SemaphoreType.DMA((1,)), pltpu.VMEM((1, 1), jnp.int32)],
        flops,
        "local",
    )
    returned = backward(next_here)
    weights, dprob, stats = call(
        partial_kernel,
        (bias, query, dout, other_own),
        (fast,) * 4,
        ((fast, (length, lanes), f32), (fast, (length, lanes), f32), (fast, (8, lanes), f32)),
        [],
        flops // 4,
        "partial",
    )
    next_there, term_there, dscore = call(
        remote_kernel,
        (bias, query, dout, other_prev, weights, dprob, stats),
        (fast,) * 7,
        ((fast, (rows, half), bf16), (fast, (rows, half), bf16), (fast, (rows, lanes), bf16)),
        [],
        flops,
        "remote",
    )
    swapped = swap(term_there)
    crossed = across(next_there, -1)
    dq, total = call(
        last_kernel,
        (dscore, other_own, other_prev, term_here, returned, dq),
        (fast, fast, fast, fast, fast, anywhere),
        ((anywhere, (tokens, width), bf16), (fast, (rows, half), f32)),
        stage,
        flops,
        "last",
        {5: 0},
    )
    outs = []
    for rows in (slice(0, length), slice(length, 2 * length)):
        part = total[rows] + crossed[rows].astype(f32) + swapped[rows].astype(f32)
        outs.append(part.astype(bf16)[None, None])
    return dq[None, None], *outs


def solution(mesh):
    placed = (
        P("outer", "inner", "head", None),
        P("outer", "inner", "head", None),
        P("outer", "inner", None, "head"),
        P("outer", "inner", None, "head"),
        P("outer", "inner", None, "head"),
        P("outer", "inner", None, "head"),
        P("outer", "inner"),
    )
    return jax.shard_map(
        on_device,
        mesh=mesh,
        in_specs=placed,
        out_specs=(
            P("outer", "inner", "head", None),
            P("outer", "inner", None, "head"),
            P("outer", "inner", None, "head"),
        ),
        check_vma=False,
    )
```
